32 devices in a mesh: dp: 4 (over y, core), expert: 8 (over z, x).
Axes of the slice: x: 2, y: 2, z: 4, core: 2. Of those that a mesh axis runs over, the one named last changes fastest.
Arguments:
- route_experts: int32 [4096, 8], P(('dp', 'expert')), may hold values from 0 to 63, all different within a row; in each aligned block of 128 rows (0 to 127, 128 to 255, ...) at most 18 rows name the same one
- router_gate_weight: float32 [4096, 8], P(('dp', 'expert')), may hold values from 0.02 to 0.3
- forget_mask: int32 [4096], P(('dp', 'expert')), may hold values 0 or 1
- retain_mask: int32 [4096], P(('dp', 'expert')), may hold values 0 or 1
- layer_output: bfloat16 [4096, 3584], P(('dp', 'expert')), may hold values from -6 to 6
- frozen_output: bfloat16 [4096, 3584], P(('dp', 'expert')), may hold values from -6 to 6
- control_vector: float32 [3584], replicated, may hold values from 0.1 to 1
- saved_hidden: bfloat16 [256, 144, 2048], P(('dp', 'expert')), may hold values from -6 to 6
- adapter_in: bfloat16 [2048, 4096], P('dp', 'expert'), may hold values from -0.125 to 0.125
- adapter_out: bfloat16 [3584, 4096], P('dp', 'expert'), may hold values from -0.09375 to 0.09375
Outputs:
- grad_in: float32 [2048, 4096], P('dp', 'expert')
- grad_out: float32 [3584, 4096], P('dp', 'expert')
The draws below stay inside these ranges and needn't reach their ends.
Inputs may be any that keep to these rules, and one draw needn't show every extreme that they name: `route_experts`: each row names 8 different experts; within the 128 rows of one device no expert is named more than 18 times, a bound that some block reaches.
All inputs are finite; a program needn't handle non-finite values. No bound on the sum of `forget_mask` or of `retain_mask` on one device may be relied on, other than what follows from the above.
Results may differ from the reference program's by a relative error of at most 0.0041.
Values may be sent and summed in bfloat16 or wider, within the bound.
A program may use at most 128 MiB of HBM per device.

```python
import math
import jax
import jax.numpy as jnp
import numpy as np
from jax import lax

OUTPUT_FEATURES = 3584
FF = 2048
RANK = 64
TOP = 8
TOK_DEV = 128
EXPERTS = 64
CAP = 18
SLOTS = 144
TOKENS = 4096
N_DP = 4
N_EXPERT = 8


def place_ends(values, stream_key, low, top_value):
    place = [jax.random.randint(jax.random.fold_in(stream_key, axis), (), 0, length) for axis, length in enumerate(values.shape)]
    longest = values.shape.index(max(values.shape))
    next_to = place[:longest] + [(place[longest] + 1) % values.shape[longest]] + place[longest + 1:]
    return values.at[tuple(place)].set(low).at[tuple(next_to)].set(top_value)


def shard_levels(rng, dims, split, least, largest):
    loudness, own = 1.0, jax.random.fold_in(rng, 6)
    for dim, parts in split:
        draws = jnp.exp(jax.random.uniform(jax.random.fold_in(own, dim), (parts,), jnp.float32, least / len(split), largest / len(split)))
        loudness = loudness * jnp.repeat(draws, dims[dim] // parts).reshape([-1 if axis == dim else 1 for axis in range(len(dims))])
    return loudness


def routed_block(own_key, own, number, rows, number_of, top, reach, skew):
    sequence = jax.random.permutation(own_key, number_of)
    crowded, ordinary = load_shares(number_of, rows * top, reach, skew, True), load_shares(number_of, rows * top, reach, skew, False)
    places = jnp.arange(number_of)

    def named(lengths, rotation):
        used = int((lengths > 0).sum())
        fixed = max(1, used // 4)
        moved = fixed + (places - fixed + rotation * (used - fixed)) % max(1, number_of - fixed)
        return jnp.zeros((number_of,), jnp.int32).at[sequence[jnp.where(places < fixed, places, moved)]].set(jnp.asarray(lengths, jnp.int32))

    lengths = jnp.where(number % 4 == 0, named(crowded, number // 4), named(ordinary, number - number // 4 - 1))
    mixed = jax.random.permutation(jax.random.fold_in(own, 3), number_of)
    donor, receiver = mixed[0:number_of // 2 * 2:2], mixed[1:number_of // 2 * 2:2]
    slack = jnp.minimum(lengths[donor] - 1, reach - lengths[receiver]) // 2
    slack = jnp.where((donor == sequence[0]) | (receiver == sequence[0]) | (lengths[receiver] == 0), 0, jnp.maximum(slack, 0))
    moved = jax.random.randint(jax.random.fold_in(own, 4), (number_of // 2,), 0, 1 << 20) % (slack + 1)
    lengths = lengths.at[donor].add(-moved).at[receiver].add(moved)
    items = jnp.searchsorted(jnp.cumsum(lengths), jnp.arange(rows * top), side="right").astype(jnp.int32)
    grid = items.reshape(top, rows).T
    grid = grid[jax.random.permutation(jax.random.fold_in(own, 1), rows)]
    rotation = jax.random.randint(jax.random.fold_in(own, 2), (rows, 1), 0, top)
    return jnp.take_along_axis(grid, (jnp.arange(top)[None, :] + rotation) % top, axis=1)


def load_shares(count, total, most, slope, full):
    weights = [(1 << 20) // math.isqrt(grade ** slope) + 1 for grade in range(1, count + 1)]
    largest = most if full else min(most, max(-(-total // count), total * weights[0] // sum(weights)))
    least = 1 if total - largest >= count - 1 else 0
    given, spare = [largest] + [least] * (count - 1), total - largest - least * (count - 1)
    while spare > 0:
        free = [i for i in range(1, count) if given[i] < largest] or [i for i in range(1, count) if given[i] < most]
        mass, left = sum([weights[i] for i in free]), spare
        for i in free:
            extra = min(most - given[i], max(1, left * weights[i] // mass), spare)
            given[i] = given[i] + extra
            spare = spare - extra
    return np.array(given)


def scatter_about(rng, extent, deviation, bound, cuts=(), kind=jnp.bfloat16):
    factor_of = shard_levels(rng, extent, cuts, -0.22, 0.18) if cuts else 1.0
    entries = jax.random.normal(rng, extent, jnp.float32) * deviation * factor_of
    return jnp.minimum(jnp.maximum(entries, -bound), bound).astype(kind)


def setup_inputs(seed: int = 0) -> dict:
    key_list = jax.random.split(jax.random.key(seed), 11)
    route_experts_keys = jax.random.split(jax.random.fold_in(key_list[0], 1), TOKENS // TOK_DEV)
    route_experts_turns = jax.random.permutation(jax.random.fold_in(key_list[0], 3), TOKENS // TOK_DEV)
    route_experts = jax.vmap(lambda own, number: routed_block(jax.random.fold_in(key_list[0], 2), own, number, TOK_DEV, EXPERTS, TOP, CAP, 2))(route_experts_keys, route_experts_turns).reshape((TOKENS, TOP))
    router_gate_weight = jnp.clip(0.02 + 0.28 * jax.random.uniform(key_list[1], (TOKENS, TOP), jnp.float32) ** shard_levels(key_list[1], (TOKENS, TOP), ((0, 32),), -0.2, 0.2), 0.02, 0.3)
    forget_mask = place_ends((jax.random.randint(key_list[2], (TOKENS,), 0, 2) < 1).astype(jnp.int32), jax.random.fold_in(key_list[2], 1), 0, 1)
    retain_mask = place_ends((jax.random.randint(key_list[3], (TOKENS,), 0, 2) < 1).astype(jnp.int32), jax.random.fold_in(key_list[3], 1), 0, 1)
    layer_output = scatter_about(key_list[4], (TOKENS, OUTPUT_FEATURES), 1.0, 6.0, ((0, 32),))
    frozen_output = scatter_about(key_list[5], (TOKENS, OUTPUT_FEATURES), 1.0, 6.0, ((0, 32),))
    control_vector = jnp.clip(jax.random.uniform(key_list[6], (OUTPUT_FEATURES,), jnp.float32, 0.1, 1.0), 0.1, 1.0)
    saved_hidden = scatter_about(key_list[7], (N_DP * EXPERTS, SLOTS, FF), 1.0, 6.0, ((0, 32),))
    adapter_in = scatter_about(key_list[8], (FF, EXPERTS * RANK), FF ** -0.5, 0.125, ((0, 4), (1, 8)))
    adapter_out = scatter_about(key_list[9], (OUTPUT_FEATURES, EXPERTS * RANK), OUTPUT_FEATURES ** -0.5, 0.09375, ((0, 4), (1, 8)))
    return dict(route_experts=route_experts, router_gate_weight=router_gate_weight, forget_mask=forget_mask, retain_mask=retain_mask, layer_output=layer_output, frozen_output=frozen_output, control_vector=control_vector, saved_hidden=saved_hidden, adapter_in=adapter_in, adapter_out=adapter_out)


steer_coef = 20.0
retain_weight = 1.5
adapter_scale_factor = 2.0
grad_coef = 0.0625

def route_slots(experts_flat, count_all, capacity):
    onehot = (experts_flat[:, None] == jnp.arange(count_all, dtype=jnp.int32)[None, :]).astype(jnp.int32)
    running = jnp.cumsum(onehot, axis=0) - 1
    within = lax.optimization_barrier(jnp.sum(onehot * running, axis=1))
    return (experts_flat * capacity + within).astype(jnp.int32)

def token_cotangent(layer_output, frozen_output, forget_mask, retain_mask, control_vector):
    unit = control_vector / jnp.sqrt(jnp.sum(control_vector * control_vector))
    current = layer_output.astype(jnp.float32)
    forget_term = current - steer_coef * unit[None, :]
    retain_term = current - frozen_output.astype(jnp.float32)
    forget_weight = forget_mask.astype(jnp.float32)[:, None]
    retain_part = retain_mask.astype(jnp.float32)[:, None]
    return grad_coef * (forget_weight * forget_term + retain_weight * retain_part * retain_term)

def reference(route_experts, router_gate_weight, forget_mask, retain_mask, layer_output, frozen_output, control_vector, saved_hidden, adapter_in, adapter_out):
    input_adapter_factor = adapter_in.astype(jnp.float32).reshape(FF, EXPERTS, RANK)
    factor_out = adapter_out.astype(jnp.float32).reshape(OUTPUT_FEATURES, EXPERTS, RANK)

    def visit(carry, block):
        grad_in, grad_out = carry
        row_dp = (block // N_EXPERT).astype(jnp.int32)
        row_ex = (block % N_EXPERT).astype(jnp.int32)
        first = (block * TOK_DEV).astype(jnp.int32)
        experts_flat = lax.dynamic_slice_in_dim(route_experts, first, TOK_DEV, 0).reshape(-1)
        gate_block_slice = lax.dynamic_slice_in_dim(router_gate_weight, first, TOK_DEV, 0)
        output_gradient = token_cotangent(lax.dynamic_slice_in_dim(layer_output, first, TOK_DEV, 0), lax.dynamic_slice_in_dim(frozen_output, first, TOK_DEV, 0), lax.dynamic_slice_in_dim(forget_mask, first, TOK_DEV, 0), lax.dynamic_slice_in_dim(retain_mask, first, TOK_DEV, 0), control_vector)
        value_rows = (gate_block_slice[:, :, None] * adapter_scale_factor * output_gradient[:, None, :]).reshape(-1, OUTPUT_FEATURES).astype(jnp.bfloat16)
        expert_slot_index = route_slots(experts_flat, EXPERTS, CAP)
        cube = jnp.zeros((EXPERTS * CAP, OUTPUT_FEATURES), jnp.bfloat16).at[expert_slot_index].set(value_rows).reshape(EXPERTS, CAP, OUTPUT_FEATURES)
        zero_index = jnp.zeros((), jnp.int32)
        hidden = lax.dynamic_slice(saved_hidden, (row_dp * EXPERTS, row_ex * CAP, zero_index), (EXPERTS, CAP, FF))
        hidden_wide = hidden.astype(jnp.float32)
        cube_wide = cube.astype(jnp.float32)
        codes = jnp.einsum('esf,fer->esr', hidden_wide, input_adapter_factor).astype(jnp.bfloat16)
        back = jnp.einsum('esd,der->esr', cube_wide, factor_out).astype(jnp.bfloat16)
        grad_in = grad_in + jnp.einsum('esf,esr->fer', hidden_wide, back.astype(jnp.float32))
        grad_out = grad_out + jnp.einsum('esd,esr->der', cube_wide, codes.astype(jnp.float32))
        return ((grad_in, grad_out), None)
    start = (jnp.zeros((FF, EXPERTS, RANK), jnp.float32), jnp.zeros((OUTPUT_FEATURES, EXPERTS, RANK), jnp.float32))
    blocks = jnp.arange(N_DP * N_EXPERT, dtype=jnp.int32)
    (grad_in, grad_out), unused = lax.scan(visit, start, blocks)
    return (grad_in.reshape(FF, EXPERTS * RANK), grad_out.reshape(OUTPUT_FEATURES, EXPERTS * RANK))
```

```python
import functools

import jax
import jax.numpy as jnp
from jax import lax
from jax.experimental import pallas as pl
from jax.experimental.pallas import tpu as pltpu
from jax.sharding import PartitionSpec as P

steer_coef = 20.0
retain_weight = 1.5
adapter_scale_factor = 2.0
grad_coef = 0.0625

F32 = jnp.float32
BF16 = jnp.bfloat16


def token_cotangent(layer_output, frozen_output, forget_mask, retain_mask, control_vector):
    unit = control_vector / jnp.sqrt(jnp.sum(control_vector * control_vector))
    current = layer_output.astype(F32)
    forget_term = current - steer_coef * unit[None, :]
    retain_term = current - frozen_output.astype(F32)
    forget_weight = forget_mask.astype(F32)[:, None]
    retain_part = retain_mask.astype(F32)[:, None]
    return grad_coef * (forget_weight * forget_term + retain_weight * retain_part * retain_term)


def expand_gate(gate, experts_here, width):
    rank = width // experts_here
    row = lax.broadcasted_iota(jnp.int32, (experts_here, width), 0)
    column = lax.broadcasted_iota(jnp.int32, (experts_here, width), 1)
    spread = ((column >= row * rank) & (column < (row + 1) * rank)).astype(F32)
    return jnp.dot(gate, spread, precision=lax.Precision.HIGHEST, preferred_element_type=F32)


def block_mask(rows, width, experts_here):
    per_row, per_column = rows // experts_here, width // experts_here
    row = lax.broadcasted_iota(jnp.int32, (rows, width), 0)
    column = lax.broadcasted_iota(jnp.int32, (rows, width), 1)
    mask = jnp.zeros((rows, width), jnp.bool_)
    for e in range(experts_here):
        mask |= (
            (row >= e * per_row)
            & (row < (e + 1) * per_row)
            & (column >= e * per_column)
            & (column < (e + 1) * per_column)
        )
    return mask


def project_kernel(experts_here, cot_ref, out_factor_ref, pick_ref, gate_ref, back_ref):
    data, tokens, depth = cot_ref.shape[1:]
    width = out_factor_ref.shape[1]
    rows = pick_ref.shape[-1]
    rank = width // experts_here
    coded = jnp.dot(
        cot_ref[0].reshape(data * tokens, depth), out_factor_ref[...], preferred_element_type=F32
    )
    mask = block_mask(rows, width, experts_here)
    for p in range(data):
        scaled = coded[p * tokens : (p + 1) * tokens] * expand_gate(
            gate_ref[0, p], experts_here, width
        )
        high = scaled.astype(BF16)
        low = (scaled - high.astype(F32)).astype(BF16)
        pick = pick_ref[0, p]
        dims = (((0,), (0,)), ((), ()))
        chosen = lax.dot_general(pick, high, dims, preferred_element_type=F32)
        chosen += lax.dot_general(pick, low, dims, preferred_element_type=F32)
        chosen = jnp.where(mask, chosen, 0.0)
        total = chosen[:, :rank]
        for e in range(1, experts_here):
            total += chosen[:, e * rank : (e + 1) * rank]
        back_ref[p, 0] = total


def outer_kernel(experts_here, cot_ref, codes_ref, pick_ref, gate_ref, grad_ref):
    data, tokens, depth = cot_ref.shape[1:]
    width = grad_ref.shape[1]
    rows = pick_ref.shape[-1]
    mask = block_mask(rows, width, experts_here)

    @pl.when(pl.program_id(0) == 0)
    def _():
        grad_ref[...] = jnp.zeros_like(grad_ref)

    parts = []
    for p in range(data):
        codes = codes_ref[p, 0].astype(F32)
        wide = jnp.where(mask, jnp.concatenate([codes] * experts_here, axis=1), 0.0).astype(BF16)
        laid = jnp.dot(pick_ref[0, p], wide, preferred_element_type=F32)
        parts.append((laid * expand_gate(gate_ref[0, p], experts_here, width)).astype(BF16))
    laid = jnp.concatenate(parts, axis=0)
    grad_ref[...] += lax.dot_general(
        cot_ref[0].reshape(data * tokens, depth),
        laid,
        (((0,), (0,)), ((), ())),
        preferred_element_type=F32,
    )


def local(
    route_experts,
    router_gate_weight,
    forget_mask,
    retain_mask,
    layer_output,
    frozen_output,
    control_vector,
    saved_hidden,
    adapter_in,
    adapter_out,
):
    experts_here, slot_count, hidden_width = saved_hidden.shape
    tokens, feature_width = layer_output.shape
    top = route_experts.shape[1]
    width = adapter_in.shape[1]
    rank = width // experts_here
    along = lax.axis_size("expert")
    data = lax.axis_size("dp")
    capacity = slot_count // along
    rows = experts_here * capacity
    depth = feature_width // data

    info = jnp.concatenate([route_experts.astype(F32), router_gate_weight], axis=1)
    info = lax.all_gather(info, ("dp", "expert"), axis=0, tiled=False)
    info = info.reshape(data, along, tokens, 2 * top).transpose(1, 0, 2, 3)
    first = lax.axis_index("expert") * experts_here
    mine = (first + jnp.arange(experts_here, dtype=jnp.int32)).astype(F32)
    named = info[..., :top, None] == mine
    gate = adapter_scale_factor * jnp.sum(
        jnp.where(named, info[..., top:, None], 0.0), axis=3
    )
    member = jnp.any(named, axis=3)
    earlier = jnp.tril(jnp.ones((tokens, tokens), BF16), -1)
    place = jnp.einsum(
        "ut,ipte->ipue", earlier, member.astype(BF16), preferred_element_type=F32
    )
    place = jnp.where(member, place, -1.0)
    pick = (
        (place[..., None] == jnp.arange(capacity, dtype=jnp.int32).astype(F32))
        .astype(BF16)
        .reshape(along, data, tokens, rows)
    )

    cotangent = token_cotangent(
        layer_output, frozen_output, forget_mask, retain_mask, control_vector
    ).astype(BF16)
    cotangent = cotangent.reshape(tokens, data, depth).transpose(1, 0, 2)
    cotangent = lax.all_to_all(cotangent, "dp", split_axis=0, concat_axis=0, tiled=True)
    cotangent = lax.all_gather(cotangent, "expert", axis=0, tiled=False)

    in_factor = lax.all_gather(adapter_in, "dp", axis=0, tiled=True)
    codes = jnp.einsum(
        "esf,fer->esr",
        saved_hidden,
        in_factor.reshape(hidden_width, experts_here, rank),
        preferred_element_type=F32,
    ).astype(BF16)
    codes = codes.reshape(experts_here, along, capacity, rank).transpose(1, 0, 2, 3)
    codes = lax.all_gather(codes.reshape(along, rows, rank), "dp", axis=0, tiled=False)

    cot_spec = pl.BlockSpec((1, data, tokens, depth), lambda i: (i, 0, 0, 0))
    pick_spec = pl.BlockSpec((1, data, tokens, rows), lambda i: (i, 0, 0, 0))
    gate_spec = pl.BlockSpec((1, data, tokens, experts_here), lambda i: (i, 0, 0, 0))
    slot_spec = pl.BlockSpec((data, 1, rows, rank), lambda i: (0, i, 0, 0))
    params = pltpu.CompilerParams(vmem_limit_bytes=40 * 1024 * 1024)
    cost = pl.CostEstimate(
        flops=2 * along * data * tokens * depth * width,
        bytes_accessed=2 * along * data * tokens * depth,
        transcendentals=0,
    )
    back = pl.pallas_call(
        functools.partial(project_kernel, experts_here),
        grid=(along,),
        in_specs=[
            cot_spec,
            pl.BlockSpec((depth, width), lambda i: (0, 0)),
            pick_spec,
            gate_spec,
        ],
        out_specs=slot_spec,
        out_shape=jax.ShapeDtypeStruct((data, along, rows, rank), F32),
        compiler_params=params,
        cost_estimate=cost,
        name="project",
    )(cotangent, adapter_out, pick, gate)
    back = lax.psum_scatter(back, "dp", scatter_dimension=0, tiled=False)
    back = (
        back.astype(BF16)
        .reshape(along, experts_here, capacity, rank)
        .transpose(1, 0, 2, 3)
        .reshape(experts_here, slot_count, rank)
    )
    grad_out = pl.pallas_call(
        functools.partial(outer_kernel, experts_here),
        grid=(along,),
        in_specs=[cot_spec, slot_spec, pick_spec, gate_spec],
        out_specs=pl.BlockSpec((depth, width), lambda i: (0, 0)),
        out_shape=jax.ShapeDtypeStruct((depth, width), F32),
        compiler_params=params,
        cost_estimate=cost,
        name="outer",
    )(cotangent, codes, pick, gate)
    product = jnp.einsum("esf,esr->fer", saved_hidden, back, preferred_element_type=F32)
    grad_in = lax.psum_scatter(
        product.reshape(hidden_width, width), "dp", scatter_dimension=0, tiled=True
    )
    return (grad_in, grad_out)


def solution(mesh):
    return jax.shard_map(
        local,
        mesh=mesh,
        in_specs=(
            P(("dp", "expert"), None),
            P(("dp", "expert"), None),
            P(("dp", "expert")),
            P(("dp", "expert")),
            P(("dp", "expert"), None),
            P(("dp", "expert"), None),
            P(),
            P(("dp", "expert"), None, None),
            P("dp", "expert"),
            P("dp", "expert"),
        ),
        out_specs=(P("dp", "expert"), P("dp", "expert")),
        check_vma=False,
    )
```

```python
import functools

import jax
import jax.numpy as jnp
from jax import lax
from jax.experimental import pallas as pl
from jax.experimental.pallas import tpu as pltpu
from jax.sharding import PartitionSpec as P

steer_coef = 20.0
retain_weight = 1.5
adapter_scale_factor = 2.0
grad_coef = 0.0625

F32 = jnp.float32
BF16 = jnp.bfloat16


def token_cotangent(layer_output, frozen_output, forget_mask, retain_mask, control_vector):
    unit = control_vector / jnp.sqrt(jnp.sum(control_vector * control_vector))
    current = layer_output.astype(F32)
    forget_term = current - steer_coef * unit[None, :]
    retain_term = current - frozen_output.astype(F32)
    forget_weight = forget_mask.astype(F32)[:, None]
    retain_part = retain_mask.astype(F32)[:, None]
    return grad_coef * (forget_weight * forget_term + retain_weight * retain_part * retain_term)


def block_mask(rows, width, experts_here):
    per_row, per_column = rows // experts_here, width // experts_here
    row = lax.broadcasted_iota(jnp.int32, (rows, width), 0)
    column = lax.broadcasted_iota(jnp.int32, (rows, width), 1)
    mask = jnp.zeros((rows, width), jnp.bool_)
    for e in range(experts_here):
        mask |= (
            (row >= e * per_row)
            & (row < (e + 1) * per_row)
            & (column >= e * per_column)
            & (column < (e + 1) * per_column)
        )
    return mask


def project_kernel(experts_here, cot_ref, out_factor_ref, pick_ref, back_ref):
    data, tokens, depth = cot_ref.shape[1:]
    width = out_factor_ref.shape[1]
    rows = pick_ref.shape[-1]
    rank = width // experts_here
    coded = jnp.dot(
        cot_ref[0].reshape(data * tokens, depth), out_factor_ref[...], preferred_element_type=F32
    )
    mask = block_mask(rows, width, experts_here)
    for p in range(data):
        own = coded[p * tokens : (p + 1) * tokens]
        high = own.astype(BF16)
        low = (own - high.astype(F32)).astype(BF16)
        pick = pick_ref[0, p]
        dims = (((0,), (0,)), ((), ()))
        chosen = lax.dot_general(pick, high, dims, preferred_element_type=F32)
        chosen += lax.dot_general(pick, low, dims, preferred_element_type=F32)
        chosen = jnp.where(mask, chosen, 0.0)
        total = chosen[:, :rank]
        for e in range(1, experts_here):
            total += chosen[:, e * rank : (e + 1) * rank]
        back_ref[p, 0] = total


def outer_kernel(experts_here, cot_ref, codes_ref, pick_ref, grad_ref):
    data, tokens, depth = cot_ref.shape[1:]
    width = grad_ref.shape[1]
    rows = pick_ref.shape[-1]
    mask = block_mask(rows, width, experts_here)

    @pl.when(pl.program_id(0) == 0)
    def _():
        grad_ref[...] = jnp.zeros_like(grad_ref)

    parts = []
    for p in range(data):
        codes = codes_ref[p, 0].astype(F32)
        wide = jnp.where(mask, jnp.concatenate([codes] * experts_here, axis=1), 0.0).astype(BF16)
        laid = jnp.dot(pick_ref[0, p], wide, preferred_element_type=F32)
        parts.append(laid.astype(BF16))
    laid = jnp.concatenate(parts, axis=0)
    grad_ref[...] += lax.dot_general(
        cot_ref[0].reshape(data * tokens, depth),
        laid,
        (((0,), (0,)), ((), ())),
        preferred_element_type=F32,
    )


def sum_over_data(terms, wire):
    data = terms.shape[0]
    core = lax.axis_index("dp") % 2
    pairs = terms.reshape((data // 2, 2) + terms.shape[1:])
    theirs = lax.dynamic_index_in_dim(pairs, 1 - core, 1, keepdims=False)
    kept = lax.dynamic_index_in_dim(pairs, core, 1, keepdims=False)
    kept = kept + lax.ppermute(theirs, "dp", [(i, i ^ 1) for i in range(data)])
    groups = [list(range(c, data, 2)) for c in range(2)]
    landed = lax.all_to_all(
        kept.astype(wire), "dp", split_axis=0, concat_axis=0, axis_index_groups=groups, tiled=True
    )
    return jnp.sum(landed.astype(F32), axis=0)


def local(
    route_experts,
    router_gate_weight,
    forget_mask,
    retain_mask,
    layer_output,
    frozen_output,
    control_vector,
    saved_hidden,
    adapter_in,
    adapter_out,
):
    experts_here, slot_count, hidden_width = saved_hidden.shape
    tokens, feature_width = layer_output.shape
    top = route_experts.shape[1]
    width = adapter_in.shape[1]
    rank = width // experts_here
    along = lax.axis_size("expert")
    data = lax.axis_size("dp")
    capacity = slot_count // along
    rows = experts_here * capacity
    depth = feature_width // data

    info = jnp.concatenate([route_experts.astype(F32), router_gate_weight], axis=1)
    info = lax.all_gather(info, ("dp", "expert"), axis=0, tiled=False)
    info = info.reshape(data, along, tokens, 2 * top).transpose(1, 0, 2, 3)
    first = lax.axis_index("expert") * experts_here
    mine = (first + jnp.arange(experts_here, dtype=jnp.int32)).astype(F32)
    named = info[..., :top, None] == mine
    gate = adapter_scale_factor * jnp.sum(
        jnp.where(named, info[..., top:, None], 0.0), axis=3
    )
    member = jnp.any(named, axis=3)
    earlier = jnp.tril(jnp.ones((tokens, tokens), BF16), -1)
    place = jnp.einsum(
        "ut,ipte->ipue", earlier, member.astype(BF16), preferred_element_type=F32
    )
    place = jnp.where(member, place, -1.0)
    pick = (
        (place[..., None] == jnp.arange(capacity, dtype=jnp.int32).astype(F32))
        .astype(BF16)
        .reshape(along, data, tokens, rows)
    )

    slot_gate = jnp.sum(
        jnp.where(
            place[..., None] == jnp.arange(capacity, dtype=jnp.int32).astype(F32),
            gate[..., None],
            0.0,
        ),
        axis=2,
    ).reshape(along, data, rows, 1)

    cotangent = token_cotangent(
        layer_output, frozen_output, forget_mask, retain_mask, control_vector
    ).astype(BF16)
    cotangent = cotangent.reshape(tokens, data, depth).transpose(1, 0, 2)
    cotangent = lax.all_to_all(cotangent, "dp", split_axis=0, concat_axis=0, tiled=True)
    in_factor = lax.all_gather(adapter_in, "dp", axis=0, tiled=True)
    cotangent, in_factor = lax.optimization_barrier((cotangent, in_factor))
    cotangent = lax.all_gather(cotangent, "expert", axis=0, tiled=False)

    codes = jnp.einsum(
        "esf,fer->esr",
        saved_hidden,
        in_factor.reshape(hidden_width, experts_here, rank),
        preferred_element_type=F32,
    ).astype(BF16)
    codes = codes.reshape(experts_here, along, capacity, rank).transpose(1, 0, 2, 3)
    codes = lax.all_gather(codes.reshape(along, rows, rank), "dp", axis=0, tiled=False)
    codes = (codes.astype(F32) * slot_gate.transpose(1, 0, 2, 3)).astype(BF16)
    cotangent, codes = lax.optimization_barrier((cotangent, codes))

    cot_spec = pl.BlockSpec((1, data, tokens, depth), lambda i: (i, 0, 0, 0))
    pick_spec = pl.BlockSpec((1, data, tokens, rows), lambda i: (i, 0, 0, 0))
    slot_spec = pl.BlockSpec((data, 1, rows, rank), lambda i: (0, i, 0, 0))
    params = pltpu.CompilerParams(vmem_limit_bytes=40 * 1024 * 1024)
    cost = pl.CostEstimate(
        flops=2 * along * data * tokens * depth * width,
        bytes_accessed=2 * along * data * tokens * depth,
        transcendentals=0,
    )
    back = pl.pallas_call(
        functools.partial(project_kernel, experts_here),
        grid=(along,),
        in_specs=[
            cot_spec,
            pl.BlockSpec((depth, width), lambda i: (0, 0)),
            pick_spec,
        ],
        out_specs=slot_spec,
        out_shape=jax.ShapeDtypeStruct((data, along, rows, rank), F32),
        compiler_params=params,
        cost_estimate=cost,
        name="project",
    )(cotangent, adapter_out, pick)
    back = sum_over_data(back, F32)
    own_gate = lax.dynamic_index_in_dim(slot_gate, lax.axis_index("dp"), 1, keepdims=False)
    back = (
        (back * own_gate)
        .astype(BF16)
        .reshape(along, experts_here, capacity, rank)
        .transpose(1, 0, 2, 3)
        .reshape(experts_here, slot_count, rank)
    )
    grad_out = pl.pallas_call(
        functools.partial(outer_kernel, experts_here),
        grid=(along,),
        in_specs=[cot_spec, slot_spec, pick_spec],
        out_specs=pl.BlockSpec((depth, width), lambda i: (0, 0)),
        out_shape=jax.ShapeDtypeStruct((depth, width), F32),
        compiler_params=params,
        cost_estimate=cost,
        name="outer",
    )(cotangent, codes, pick)
    product = jnp.einsum("esf,esr->fer", saved_hidden, back, preferred_element_type=F32)
    grad_in = sum_over_data(product.reshape(data, hidden_width // data, width), BF16)
    return (grad_in, grad_out)


def solution(mesh):
    return jax.shard_map(
        local,
        mesh=mesh,
        in_specs=(
            P(("dp", "expert"), None),
            P(("dp", "expert"), None),
            P(("dp", "expert")),
            P(("dp", "expert")),
            P(("dp", "expert"), None),
            P(("dp", "expert"), None),
            P(),
            P(("dp", "expert"), None, None),
            P("dp", "expert"),
            P("dp", "expert"),
        ),
        out_specs=(P("dp", "expert"), P("dp", "expert")),
        check_vma=False,
    )
```

```python
import functools

import jax
import jax.numpy as jnp
from jax import lax
from jax.experimental import pallas as pl
from jax.experimental.pallas import tpu as pltpu
from jax.sharding import PartitionSpec as P

steer_coef = 20.0
retain_weight = 1.5
adapter_scale_factor = 2.0
grad_coef = 0.0625

F32 = jnp.float32
BF16 = jnp.bfloat16


def token_cotangent(layer_output, frozen_output, forget_mask, retain_mask, control_vector):
    unit = control_vector / jnp.sqrt(jnp.sum(control_vector * control_vector))
    current = layer_output.astype(F32)
    forget_term = current - steer_coef * unit[None, :]
    retain_term = current - frozen_output.astype(F32)
    forget_weight = forget_mask.astype(F32)[:, None]
    retain_part = retain_mask.astype(F32)[:, None]
    return grad_coef * (forget_weight * forget_term + retain_weight * retain_part * retain_term)


def block_mask(rows, width, experts_here):
    per_row, per_column = rows // experts_here, width // experts_here
    row = lax.broadcasted_iota(jnp.int32, (rows, width), 0)
    column = lax.broadcasted_iota(jnp.int32, (rows, width), 1)
    mask = jnp.zeros((rows, width), jnp.bool_)
    for e in range(experts_here):
        mask |= (
            (row >= e * per_row)
            & (row < (e + 1) * per_row)
            & (column >= e * per_column)
            & (column < (e + 1) * per_column)
        )
    return mask


def project_kernel(experts_here, cot_ref, out_factor_ref, pick_ref, back_ref):
    data, tokens, depth = cot_ref.shape[1:]
    width = out_factor_ref.shape[1]
    rows = pick_ref.shape[-1]
    rank = width // experts_here
    coded = jnp.dot(
        cot_ref[0].reshape(data * tokens, depth), out_factor_ref[...], preferred_element_type=F32
    )
    mask = block_mask(rows, width, experts_here)
    for p in range(data):
        own = coded[p * tokens : (p + 1) * tokens]
        high = own.astype(BF16)
        low = (own - high.astype(F32)).astype(BF16)
        pick = pick_ref[0, p]
        dims = (((0,), (0,)), ((), ()))
        chosen = lax.dot_general(pick, high, dims, preferred_element_type=F32)
        chosen += lax.dot_general(pick, low, dims, preferred_element_type=F32)
        chosen = jnp.where(mask, chosen, 0.0)
        total = chosen[:, :rank]
        for e in range(1, experts_here):
            total += chosen[:, e * rank : (e + 1) * rank]
        back_ref[p, 0] = jnp.concatenate([total[: rows // 2], total[rows // 2 :]], axis=1)


def inner_kernel(hidden_ref, back_ref, grad_ref):
    grad_ref[...] = jnp.concatenate(
        [
            lax.dot_general(
                hidden_ref[k], back_ref[k], (((0,), (0,)), ((), ())), preferred_element_type=F32
            )
            for k in range(hidden_ref.shape[0])
        ],
        axis=1,
    )


def outer_kernel(experts_here, cot_ref, codes_ref, pick_ref, grad_ref):
    data, tokens, depth = cot_ref.shape[1:]
    width = grad_ref.shape[1]
    rows = pick_ref.shape[-1]
    mask = block_mask(rows, width, experts_here)

    @pl.when(pl.program_id(0) == 0)
    def _():
        grad_ref[...] = jnp.zeros_like(grad_ref)

    parts = []
    for p in range(data):
        codes = codes_ref[p, 0].astype(F32)
        wide = jnp.where(mask, jnp.concatenate([codes] * experts_here, axis=1), 0.0).astype(BF16)
        laid = jnp.dot(pick_ref[0, p], wide, preferred_element_type=F32)
        parts.append(laid.astype(BF16))
    laid = jnp.concatenate(parts, axis=0)
    grad_ref[...] += lax.dot_general(
        cot_ref[0].reshape(data * tokens, depth),
        laid,
        (((0,), (0,)), ((), ())),
        preferred_element_type=F32,
    )


def sum_over_data(terms, wire):
    data = terms.shape[0]
    core = lax.axis_index("dp") % 2
    pairs = terms.reshape((data // 2, 2) + terms.shape[1:])
    theirs = lax.dynamic_index_in_dim(pairs, 1 - core, 1, keepdims=False)
    kept = lax.dynamic_index_in_dim(pairs, core, 1, keepdims=False)
    kept = kept + lax.ppermute(theirs, "dp", [(i, i ^ 1) for i in range(data)])
    groups = [list(range(c, data, 2)) for c in range(2)]
    landed = lax.all_to_all(
        kept.astype(wire), "dp", split_axis=0, concat_axis=0, axis_index_groups=groups, tiled=True
    )
    return jnp.sum(landed.astype(F32), axis=0)


def gather_rows(shard):
    data = lax.axis_size("dp")
    me = lax.axis_index("dp")
    pieces = [shard] + [
        lax.ppermute(shard, "dp", [((i + k) % data, i) for i in range(data)])
        for k in range(1, data)
    ]
    start = lax.rem(data - me, data) * shard.shape[0]
    twice = jnp.concatenate(pieces + pieces[:-1], axis=0)
    return lax.dynamic_slice_in_dim(twice, start, data * shard.shape[0], axis=0)


def local(
    route_experts,
    router_gate_weight,
    forget_mask,
    retain_mask,
    layer_output,
    frozen_output,
    control_vector,
    saved_hidden,
    adapter_in,
    adapter_out,
):
    experts_here, slot_count, hidden_width = saved_hidden.shape
    tokens, feature_width = layer_output.shape
    top = route_experts.shape[1]
    width = adapter_in.shape[1]
    rank = width // experts_here
    along = lax.axis_size("expert")
    data = lax.axis_size("dp")
    capacity = slot_count // along
    rows = experts_here * capacity
    depth = feature_width // data

    info = jnp.concatenate([route_experts.astype(F32), router_gate_weight], axis=1)
    info = lax.all_gather(info, ("dp", "expert"), axis=0, tiled=False)
    info = info.reshape(data, along, tokens, 2 * top).transpose(1, 0, 2, 3)
    first = lax.axis_index("expert") * experts_here
    mine = (first + jnp.arange(experts_here, dtype=jnp.int32)).astype(F32)
    named = info[..., :top, None] == mine
    gate = adapter_scale_factor * jnp.sum(
        jnp.where(named, info[..., top:, None], 0.0), axis=3
    )
    member = jnp.any(named, axis=3)
    earlier = jnp.tril(jnp.ones((tokens, tokens), BF16), -1)
    place = jnp.einsum(
        "ut,ipte->ipue", earlier, member.astype(BF16), preferred_element_type=F32
    )
    place = jnp.where(member, place, -1.0)
    pick = (
        (place[..., None] == jnp.arange(capacity, dtype=jnp.int32).astype(F32))
        .astype(BF16)
        .reshape(along, data, tokens, rows)
    )

    slot_gate = jnp.sum(
        jnp.where(
            place[..., None] == jnp.arange(capacity, dtype=jnp.int32).astype(F32),
            gate[..., None],
            0.0,
        ),
        axis=2,
    ).reshape(along, data, rows, 1)

    cotangent = token_cotangent(
        layer_output, frozen_output, forget_mask, retain_mask, control_vector
    ).astype(BF16)
    cotangent = cotangent.reshape(tokens, data, depth).transpose(1, 0, 2)
    cotangent = lax.all_to_all(cotangent, "dp", split_axis=0, concat_axis=0, tiled=True)
    cotangent, adapter_in = lax.optimization_barrier((cotangent, adapter_in))
    in_factor = gather_rows(adapter_in)
    cotangent = lax.all_gather(cotangent, "expert", axis=0, tiled=False)

    codes = jnp.einsum(
        "esf,fer->esr",
        saved_hidden,
        in_factor.reshape(hidden_width, experts_here, rank),
        preferred_element_type=F32,
    ).astype(BF16)
    codes = codes.reshape(experts_here, along, capacity, rank).transpose(1, 0, 2, 3)
    codes = lax.all_gather(codes.reshape(along, rows, rank), "dp", axis=0, tiled=False)
    codes = (codes.astype(F32) * slot_gate.transpose(1, 0, 2, 3)).astype(BF16)
    cotangent, codes = lax.optimization_barrier((cotangent, codes))

    cot_spec = pl.BlockSpec((1, data, tokens, depth), lambda i: (i, 0, 0, 0))
    pick_spec = pl.BlockSpec((1, data, tokens, rows), lambda i: (i, 0, 0, 0))
    slot_spec = pl.BlockSpec((data, 1, rows, rank), lambda i: (0, i, 0, 0))
    params = pltpu.CompilerParams(vmem_limit_bytes=40 * 1024 * 1024)
    cost = pl.CostEstimate(
        flops=2 * along * data * tokens * depth * width,
        bytes_accessed=2 * along * data * tokens * depth,
        transcendentals=0,
    )
    back = pl.pallas_call(
        functools.partial(project_kernel, experts_here),
        grid=(along,),
        in_specs=[
            cot_spec,
            pl.BlockSpec((depth, width), lambda i: (0, 0)),
            pick_spec,
        ],
        out_specs=pl.BlockSpec((data, 1, rows // 2, 2 * rank), lambda i: (0, i, 0, 0)),
        out_shape=jax.ShapeDtypeStruct((data, along, rows // 2, 2 * rank), F32),
        compiler_params=params,
        cost_estimate=cost,
        name="project",
    )(cotangent, adapter_out, pick)
    back = lax.all_to_all(back, "dp", split_axis=0, concat_axis=0, tiled=True)
    back = jnp.sum(back, axis=0).reshape(along, rows // 2, 2, rank)
    back = back.transpose(0, 2, 1, 3).reshape(along, rows, rank)
    own_gate = lax.dynamic_index_in_dim(slot_gate, lax.axis_index("dp"), 1, keepdims=False)
    back = (
        (back * own_gate)
        .astype(BF16)
        .reshape(along, experts_here, capacity, rank)
        .transpose(1, 0, 2, 3)
        .reshape(experts_here, slot_count, rank)
    )
    grad_out = pl.pallas_call(
        functools.partial(outer_kernel, experts_here),
        grid=(along,),
        in_specs=[cot_spec, slot_spec, pick_spec],
        out_specs=pl.BlockSpec((depth, width), lambda i: (0, 0)),
        out_shape=jax.ShapeDtypeStruct((depth, width), F32),
        compiler_params=params,
        cost_estimate=cost,
        name="outer",
    )(cotangent, codes, pick)
    product = pl.pallas_call(
        inner_kernel,
        grid=(experts_here // 2,),
        in_specs=[
            pl.BlockSpec((2, slot_count, hidden_width), lambda i: (i, 0, 0)),
            pl.BlockSpec((2, slot_count, rank), lambda i: (i, 0, 0)),
        ],
        out_specs=pl.BlockSpec((hidden_width, 2 * rank), lambda i: (0, i)),
        out_shape=jax.ShapeDtypeStruct((hidden_width, width), F32),
        compiler_params=params,
        name="inner",
    )(saved_hidden, back)
    grad_in = sum_over_data(product.reshape(data, hidden_width // data, width), BF16)
    return (grad_in, grad_out)


def solution(mesh):
    return jax.shard_map(
        local,
        mesh=mesh,
        in_specs=(
            P(("dp", "expert"), None),
            P(("dp", "expert"), None),
            P(("dp", "expert")),
            P(("dp", "expert")),
            P(("dp", "expert"), None),
            P(("dp", "expert"), None),
            P(),
            P(("dp", "expert"), None, None),
            P("dp", "expert"),
            P("dp", "expert"),
        ),
        out_specs=(P("dp", "expert"), P("dp", "expert")),
        check_vma=False,
    )
```

```python
import functools

import jax
import jax.numpy as jnp
from jax import lax
from jax.experimental import pallas as pl
from jax.experimental.pallas import tpu as pltpu
from jax.sharding import PartitionSpec as P

steer_coef = 20.0
retain_weight = 1.5
adapter_scale_factor = 2.0
grad_coef = 0.0625

F32 = jnp.float32
BF16 = jnp.bfloat16


def token_cotangent(layer_output, frozen_output, forget_mask, retain_mask, control_vector):
    unit = control_vector / jnp.sqrt(jnp.sum(control_vector * control_vector))
    current = layer_output.astype(F32)
    forget_term = current - steer_coef * unit[None, :]
    retain_term = current - frozen_output.astype(F32)
    forget_weight = forget_mask.astype(F32)[:, None]
    retain_part = retain_mask.astype(F32)[:, None]
    return grad_coef * (forget_weight * forget_term + retain_weight * retain_part * retain_term)


def block_mask(rows, width, experts_here):
    per_row, per_column = rows // experts_here, width // experts_here
    row = lax.broadcasted_iota(jnp.int32, (rows, width), 0)
    column = lax.broadcasted_iota(jnp.int32, (rows, width), 1)
    mask = jnp.zeros((rows, width), jnp.bool_)
    for e in range(experts_here):
        mask |= (
            (row >= e * per_row)
            & (row < (e + 1) * per_row)
            & (column >= e * per_column)
            & (column < (e + 1) * per_column)
        )
    return mask


def project_kernel(experts_here, cot_ref, out_factor_ref, pick_ref, back_ref):
    data, tokens, depth = cot_ref.shape[1:]
    width = out_factor_ref.shape[1]
    rows = pick_ref.shape[-1]
    rank = width // experts_here
    coded = jnp.dot(
        cot_ref[0].reshape(data * tokens, depth), out_factor_ref[...], preferred_element_type=F32
    )
    mask = block_mask(rows, width, experts_here)
    for p in range(data):
        own = coded[p * tokens : (p + 1) * tokens]
        high = own.astype(BF16)
        low = (own - high.astype(F32)).astype(BF16)
        pick = pick_ref[0, p]
        dims = (((0,), (0,)), ((), ()))
        chosen = lax.dot_general(pick, high, dims, preferred_element_type=F32)
        chosen += lax.dot_general(pick, low, dims, preferred_element_type=F32)
        chosen = jnp.where(mask, chosen, 0.0)
        total = chosen[:, :rank]
        for e in range(1, experts_here):
            total += chosen[:, e * rank : (e + 1) * rank]
        back_ref[p, 0] = jnp.concatenate([total[: rows // 2], total[rows // 2 :]], axis=1)


def inner_kernel(hidden_ref, back_ref, grad_ref):
    grad_ref[...] = jnp.concatenate(
        [
            lax.dot_general(
                hidden_ref[k], back_ref[k], (((0,), (0,)), ((), ())), preferred_element_type=F32
            )
            for k in range(hidden_ref.shape[0])
        ],
        axis=1,
    )


def outer_kernel(experts_here, cot_ref, codes_ref, pick_ref, grad_ref):
    data, tokens, depth = cot_ref.shape[1:]
    width = grad_ref.shape[1]
    rows = pick_ref.shape[-1]
    mask = block_mask(rows, width, experts_here)

    @pl.when(pl.program_id(0) == 0)
    def _():
        grad_ref[...] = jnp.zeros_like(grad_ref)

    parts = []
    for p in range(data):
        codes = codes_ref[p, 0].astype(F32)
        wide = jnp.where(mask, jnp.concatenate([codes] * experts_here, axis=1), 0.0).astype(BF16)
        laid = jnp.dot(pick_ref[0, p], wide, preferred_element_type=F32)
        parts.append(laid.astype(BF16))
    laid = jnp.concatenate(parts, axis=0)
    grad_ref[...] += lax.dot_general(
        cot_ref[0].reshape(data * tokens, depth),
        laid,
        (((0,), (0,)), ((), ())),
        preferred_element_type=F32,
    )


def sum_over_data(terms, wire):
    data = terms.shape[0]
    core = lax.axis_index("dp") % 2
    pairs = terms.reshape((data // 2, 2) + terms.shape[1:])
    theirs = lax.dynamic_index_in_dim(pairs, 1 - core, 1, keepdims=False)
    kept = lax.dynamic_index_in_dim(pairs, core, 1, keepdims=False)
    kept = kept + lax.ppermute(theirs, "dp", [(i, i ^ 1) for i in range(data)])
    groups = [list(range(c, data, 2)) for c in range(2)]
    landed = lax.all_to_all(
        kept.astype(wire), "dp", split_axis=0, concat_axis=0, axis_index_groups=groups, tiled=True
    )
    return jnp.sum(landed.astype(F32), axis=0)


def gather_rows(shard):
    data = lax.axis_size("dp")
    me = lax.axis_index("dp")
    pieces = [shard] + [
        lax.ppermute(shard, "dp", [((i + k) % data, i) for i in range(data)])
        for k in range(1, data)
    ]
    start = lax.rem(data - me, data) * shard.shape[0]
    twice = jnp.concatenate(pieces + pieces[:-1], axis=0)
    return lax.dynamic_slice_in_dim(twice, start, data * shard.shape[0], axis=0)


def local(
    route_experts,
    router_gate_weight,
    forget_mask,
    retain_mask,
    layer_output,
    frozen_output,
    control_vector,
    saved_hidden,
    adapter_in,
    adapter_out,
):
    experts_here, slot_count, hidden_width = saved_hidden.shape
    tokens, feature_width = layer_output.shape
    top = route_experts.shape[1]
    width = adapter_in.shape[1]
    rank = width // experts_here
    along = lax.axis_size("expert")
    data = lax.axis_size("dp")
    capacity = slot_count // along
    rows = experts_here * capacity
    depth = feature_width // data

    info = jnp.concatenate([route_experts.astype(F32), router_gate_weight], axis=1)
    info = lax.all_gather(info, ("dp", "expert"), axis=0, tiled=False)
    info = info.reshape(data, along, tokens, 2 * top).transpose(1, 0, 2, 3)
    first = lax.axis_index("expert") * experts_here
    mine = (first + jnp.arange(experts_here, dtype=jnp.int32)).astype(F32)
    named = info[..., :top, None] == mine
    gate = adapter_scale_factor * jnp.sum(
        jnp.where(named, info[..., top:, None], 0.0), axis=3
    )
    member = jnp.any(named, axis=3)
    earlier = jnp.tril(jnp.ones((tokens, tokens), BF16), -1)
    place = jnp.einsum(
        "ut,ipte->ipue", earlier, member.astype(BF16), preferred_element_type=F32
    )
    place = jnp.where(member, place, -1.0)
    pick = (
        (place[..., None] == jnp.arange(capacity, dtype=jnp.int32).astype(F32))
        .astype(BF16)
        .reshape(along, data, tokens, rows)
    )

    slot_gate = jnp.sum(
        jnp.where(
            place[..., None] == jnp.arange(capacity, dtype=jnp.int32).astype(F32),
            gate[..., None],
            0.0,
        ),
        axis=2,
    ).reshape(along, data, rows, 1)

    cotangent = token_cotangent(
        layer_output, frozen_output, forget_mask, retain_mask, control_vector
    ).astype(BF16)
    cotangent = cotangent.reshape(tokens, data, depth).transpose(1, 0, 2)
    cotangent = lax.all_to_all(cotangent, "dp", split_axis=0, concat_axis=0, tiled=True)
    in_factor = gather_rows(adapter_in)
    cotangent = lax.all_gather(cotangent, "expert", axis=0, tiled=False)

    codes = jnp.einsum(
        "esf,fer->esr",
        saved_hidden,
        in_factor.reshape(hidden_width, experts_here, rank),
        preferred_element_type=F32,
    ).astype(BF16)
    codes = codes.reshape(experts_here, along, capacity, rank).transpose(1, 0, 2, 3)
    codes = lax.all_gather(codes.reshape(along, rows, rank), "dp", axis=0, tiled=False)
    codes = (codes.astype(F32) * slot_gate.transpose(1, 0, 2, 3)).astype(BF16)
    cotangent, codes = lax.optimization_barrier((cotangent, codes))

    cot_spec = pl.BlockSpec((1, data, tokens, depth), lambda i: (i, 0, 0, 0))
    pick_spec = pl.BlockSpec((1, data, tokens, rows), lambda i: (i, 0, 0, 0))
    slot_spec = pl.BlockSpec((data, 1, rows, rank), lambda i: (0, i, 0, 0))
    params = pltpu.CompilerParams(vmem_limit_bytes=40 * 1024 * 1024)
    cost = pl.CostEstimate(
        flops=2 * along * data * tokens * depth * width,
        bytes_accessed=2 * along * data * tokens * depth,
        transcendentals=0,
    )
    back = pl.pallas_call(
        functools.partial(project_kernel, experts_here),
        grid=(along,),
        in_specs=[
            cot_spec,
            pl.BlockSpec((depth, width), lambda i: (0, 0)),
            pick_spec,
        ],
        out_specs=pl.BlockSpec((data, 1, rows // 2, 2 * rank), lambda i: (0, i, 0, 0)),
        out_shape=jax.ShapeDtypeStruct((data, along, rows // 2, 2 * rank), F32),
        compiler_params=params,
        cost_estimate=cost,
        name="project",
    )(cotangent, adapter_out, pick)
    back = lax.all_to_all(back, "dp", split_axis=0, concat_axis=0, tiled=True)
    back = jnp.sum(back, axis=0).reshape(along, rows // 2, 2, rank)
    back = back.transpose(0, 2, 1, 3).reshape(along, rows, rank)
    own_gate = lax.dynamic_index_in_dim(slot_gate, lax.axis_index("dp"), 1, keepdims=False)
    back = (
        (back * own_gate)
        .astype(BF16)
        .reshape(along, experts_here, capacity, rank)
        .transpose(1, 0, 2, 3)
        .reshape(experts_here, slot_count, rank)
    )
    grad_out = pl.pallas_call(
        functools.partial(outer_kernel, experts_here),
        grid=(along,),
        in_specs=[cot_spec, slot_spec, pick_spec],
        out_specs=pl.BlockSpec((depth, width), lambda i: (0, 0)),
        out_shape=jax.ShapeDtypeStruct((depth, width), F32),
        compiler_params=params,
        cost_estimate=cost,
        name="outer",
    )(cotangent, codes, pick)
    product = pl.pallas_call(
        inner_kernel,
        grid=(experts_here // 2,),
        in_specs=[
            pl.BlockSpec((2, slot_count, hidden_width), lambda i: (i, 0, 0)),
            pl.BlockSpec((2, slot_count, rank), lambda i: (i, 0, 0)),
        ],
        out_specs=pl.BlockSpec((hidden_width, 2 * rank), lambda i: (0, i)),
        out_shape=jax.ShapeDtypeStruct((hidden_width, width), F32),
        compiler_params=params,
        name="inner",
    )(saved_hidden, back)
    grad_in = sum_over_data(product.reshape(data, hidden_width // data, width), BF16)
    return (grad_in, grad_out)


def solution(mesh):
    return jax.shard_map(
        local,
        mesh=mesh,
        in_specs=(
            P(("dp", "expert"), None),
            P(("dp", "expert"), None),
            P(("dp", "expert")),
            P(("dp", "expert")),
            P(("dp", "expert"), None),
            P(("dp", "expert"), None),
            P(),
            P(("dp", "expert"), None, None),
            P("dp", "expert"),
            P("dp", "expert"),
        ),
        out_specs=(P("dp", "expert"), P("dp", "expert")),
        check_vma=False,
    )
```
